512 devices in a mesh: tm: 32 (over y_lo, z), height: 16 (over x, y_hi, core).
Axes of the slice: x: 4, y: 8 (y_hi: 2, y_lo: 4; y = y_hi * 4 + y_lo), z: 8, core: 2. Of those that a mesh axis runs over, the one named last changes fastest.
Arguments:
- tokens: bfloat16 [256, 112, 7, 256], P('tm', 'height'), may hold values from -6 to 6
- norm_gain: float32 [256], replicated, may hold values from 0.1 to 1.9
- qkv_weight: bfloat16 [256, 768], replicated, may hold values from -0.75 to 0.75
- proj_weight: bfloat16 [256, 256], replicated, may hold values from -0.375 to 0.375
- rel_bias: float32 [8, 2535], replicated, may hold values from -4 to 320
- cotangent: bfloat16 [256, 112, 7, 256], P('tm', 'height'), may hold values from -6 to 6
Outputs:
- block_out: bfloat16 [256, 112, 7, 256], P('tm', 'height')
- token_grad: bfloat16 [256, 112, 7, 256], P('tm', 'height')
- proj_grad: float32 [256, 256], P(None, 'height')
The draws below stay inside these ranges and needn't reach their ends.
All inputs are finite; a program needn't handle non-finite values.
Results may differ from the reference program's by a relative error of at most 0.0061.
Values may be sent and summed in bfloat16 or wider, within the bound.
A program may use at most 192 MiB of HBM per device.

```python
import jax
import jax.numpy as jnp
import numpy as np
from jax import lax

C = 256
HEADS = 8
WT = 8
WH = 7
W = 7
HEAD_DIM = 32
NT = 256
NH = 112
TOKENS = 200704


def draw_rel_bias(key, part):
    key = jax.random.fold_in(key, 11)
    offset_span = 2 * WH - 1
    columns = (2 * WT - 1) * offset_span * offset_span
    return jnp.clip(jax.random.normal(key, (HEADS, columns), jnp.float32), -4.0, 4.0)


def level_of(rng, shape, cuts, least, high):
    level, own = 1.0, jax.random.fold_in(rng, 6)
    for dim, parts in cuts:
        steps = jnp.exp(jax.random.uniform(jax.random.fold_in(own, dim), (parts,), jnp.float32, least / len(cuts), high / len(cuts)))
        level = level * jnp.repeat(steps, shape[dim] // parts).reshape([-1 if axis == dim else 1 for axis in range(len(shape))])
    return level


def gaussian(rng, shape, scale, limit, shards=(), kind=jnp.bfloat16):
    loudness = level_of(rng, shape, shards, -0.22, 0.18) if shards else 1.0
    values = jax.random.normal(rng, shape, jnp.float32) * scale * loudness
    return jnp.minimum(jnp.maximum(values, -limit), limit).astype(kind)


def setup_inputs(seed: int = 0) -> dict:
    seeds = jax.random.split(jax.random.key(seed), 7)
    return {
        "tokens": gaussian(seeds[0], (NT, NH, W, C), 1.0, 6.0, ((0, 32), (1, 16))),
        "norm_gain": jnp.clip(1.0 + 0.18 * jax.random.normal(seeds[1], (C,), jnp.float32), 0.1, 1.9),
        "qkv_weight": gaussian(seeds[2], (C, 3 * C), 0.125, 0.75),
        "proj_weight": gaussian(seeds[3], (C, C), C ** -0.5, 0.375),
        "rel_bias": draw_rel_bias(jax.random.fold_in(seeds[6], 71), 0),
        "cotangent": gaussian(seeds[5], (NT, NH, W, C), 1.0, 6.0, ((0, 32), (1, 16))),
    }


epsilon = 1e-05
masked_value = -1000000000.0

def window_table(window_frames, window_rows):
    offset_span = 2 * window_rows - 1
    frame_ids = np.repeat(np.arange(window_frames), window_rows * window_rows)
    row_ids = np.tile(np.repeat(np.arange(window_rows), window_rows), window_frames)
    column_ids = np.tile(np.arange(window_rows), window_frames * window_rows)
    offsets = ((frame_ids[:, None] - frame_ids[None, :] + window_frames - 1) * offset_span + row_ids[:, None] - row_ids[None, :] + window_rows - 1) * offset_span + column_ids[:, None] - column_ids[None, :] + window_rows - 1
    return offsets.astype(np.int32)

def region_ids(count, window, shift):
    position = jnp.arange(count, dtype=jnp.int32)
    return jnp.where(position < count - window, 0, jnp.where(position < count - shift, 1, 2)).astype(jnp.int32)

def partition(grid):
    trailing = grid.shape[3:]
    pieces = grid.reshape((NT // WT, WT, NH // WH, WH, W // WH, WH) + trailing)
    axes_order = (0, 2, 4, 1, 3, 5) + tuple(range(6, 6 + len(trailing)))
    return pieces.transpose(axes_order).reshape((NT // WT, NH // WH * (W // WH), WT * WH * WH) + trailing)

def assemble(stacked):
    trailing = stacked.shape[3:]
    pieces = stacked.reshape((NT // WT, NH // WH, W // WH, WT, WH, WH) + trailing)
    axes_order = (0, 3, 1, 4, 2, 5) + tuple(range(6, 6 + len(trailing)))
    return pieces.transpose(axes_order).reshape((NT, NH, W) + trailing)

def normalize(window_x, norm_gain):
    values = window_x.astype(jnp.float32)
    centred = values - lax.optimization_barrier(jnp.mean(values, axis=-1, keepdims=True))
    inverse = lax.rsqrt(lax.optimization_barrier(jnp.mean(centred * centred, axis=-1, keepdims=True)) + epsilon)
    standard = centred * inverse
    return (values, standard, inverse, (standard * norm_gain).astype(jnp.bfloat16))

def window_pass(window_x, grad_win, same_region, bias_grid, norm_gain, qkv_weight, proj_weight):
    values, standard, inverse, normed = normalize(window_x, norm_gain)
    projected = jnp.dot(normed, qkv_weight, preferred_element_type=jnp.float32)
    queries = (projected[:, :C] * HEAD_DIM ** (-0.5)).astype(jnp.bfloat16).reshape(-1, HEADS, HEAD_DIM)
    keys_all = projected[:, C:2 * C].astype(jnp.bfloat16).reshape(-1, HEADS, HEAD_DIM)
    values_all = projected[:, 2 * C:].astype(jnp.bfloat16).reshape(-1, HEADS, HEAD_DIM)
    scores = jnp.einsum('qhd,khd->hqk', queries.astype(jnp.float32), keys_all.astype(jnp.float32)) + bias_grid
    scores = jnp.where(same_region[None], scores, masked_value)
    raised = jnp.exp(scores - lax.optimization_barrier(jnp.max(scores, axis=-1, keepdims=True)))
    softmaxed = raised / lax.optimization_barrier(jnp.sum(raised, axis=-1, keepdims=True))
    soft_low = softmaxed.astype(jnp.bfloat16)
    attended = jnp.einsum('hqk,khd->qhd', soft_low.astype(jnp.float32), values_all.astype(jnp.float32)).reshape(-1, C).astype(jnp.bfloat16)
    output = (values + jnp.dot(attended, proj_weight, preferred_element_type=jnp.float32)).astype(jnp.bfloat16)
    grad_attended = jnp.dot(grad_win, proj_weight.T, preferred_element_type=jnp.float32).astype(jnp.bfloat16).reshape(-1, HEADS, HEAD_DIM)
    grad_values = jnp.einsum('hqk,qhd->khd', soft_low.astype(jnp.float32), grad_attended.astype(jnp.float32)).astype(jnp.bfloat16)
    grad_probs = jnp.einsum('qhd,khd->hqk', grad_attended.astype(jnp.float32), values_all.astype(jnp.float32))
    grad_scores = (softmaxed * (grad_probs - lax.optimization_barrier(jnp.sum(softmaxed * grad_probs, axis=-1, keepdims=True)))).astype(jnp.bfloat16)
    grad_queries = (jnp.einsum('hqk,khd->qhd', grad_scores.astype(jnp.float32), keys_all.astype(jnp.float32)) * HEAD_DIM ** (-0.5)).astype(jnp.bfloat16)
    grad_keys = jnp.einsum('hqk,qhd->khd', grad_scores.astype(jnp.float32), queries.astype(jnp.float32)).astype(jnp.bfloat16)
    grad_joined = jnp.concatenate([grad_queries.reshape(-1, C), grad_keys.reshape(-1, C), grad_values.reshape(-1, C)], axis=1)
    grad_normed = jnp.dot(grad_joined, qkv_weight.T, preferred_element_type=jnp.float32)
    scaled = grad_normed * norm_gain
    grad_branch = inverse * (scaled - lax.optimization_barrier(jnp.mean(scaled, axis=-1, keepdims=True)) - standard * lax.optimization_barrier(jnp.mean(scaled * standard, axis=-1, keepdims=True)))
    input_grad = (grad_win.astype(jnp.float32) + grad_branch).astype(jnp.bfloat16)
    return (output, input_grad, attended)

def reference(tokens, norm_gain, qkv_weight, proj_weight, rel_bias, cotangent):
    frame_shift = WT // 2
    row_shift = WH // 2
    shifted_tokens = jnp.roll(tokens, (-frame_shift, -row_shift, -row_shift), axis=(0, 1, 2))
    shifted_grad = jnp.roll(cotangent, (-frame_shift, -row_shift, -row_shift), axis=(0, 1, 2))
    region = region_ids(NT, WT, frame_shift)[:, None, None] * 9 + region_ids(NH, WH, row_shift)[None, :, None] * 3 + region_ids(W, WH, row_shift)[None, None, :]
    bias_grid = rel_bias[:, window_table(WT, WH)]
    token_windows = partition(shifted_tokens)
    grad_windows = partition(shifted_grad)
    region_windows = partition(region[..., None])[..., 0]
    batched = jax.vmap(window_pass, in_axes=(0, 0, 0, None, None, None, None))

    def group_step(running, packed):
        token_group, grad_group, region_group = packed
        same_region = region_group[:, :, None] == region_group[:, None, :]
        outputs, input_grads, attended = batched(token_group, grad_group, same_region, bias_grid, norm_gain, qkv_weight, proj_weight)
        grad_term = lax.dot_general(attended.reshape(-1, C), grad_group.reshape(-1, C), (((0,), (0,)), ((), ())), preferred_element_type=jnp.float32)
        return (running + grad_term, (outputs, input_grads))
    running, (outputs, input_grads) = lax.scan(group_step, jnp.zeros((C, C), jnp.float32), (token_windows, grad_windows, region_windows))
    block_out = jnp.roll(assemble(outputs), (frame_shift, row_shift, row_shift), axis=(0, 1, 2))
    token_grad = jnp.roll(assemble(input_grads), (frame_shift, row_shift, row_shift), axis=(0, 1, 2))
    proj_grad = running * TOKENS ** (-0.5)
    return (block_out, token_grad, proj_grad)
```

```python
import functools

import jax
import jax.numpy as jnp
from jax import lax
from jax.experimental import pallas as pl
from jax.experimental.pallas import tpu as pltpu
from jax.sharding import PartitionSpec as P

HEADS = 8
DIM = 32
C = 256
FRAMES = 8
ROWS = 7
COLS = 7
PADDED = 8
GROUP = FRAMES * PADDED
N = ROWS * GROUP
FS = FRAMES // 2
RS = ROWS // 2
KEEP = ROWS - RS
OFFSETS = 2 * ROWS - 1
Z_SIZE = 8
MASKED = -1e9
EPSILON = 1e-5
F32 = jnp.float32
BF16 = jnp.bfloat16
MESH = pl.DeviceIdType.MESH


def dot(a, b, dims=((1,), (0,))):
    return lax.dot_general(a, b, (dims, ((), ())), preferred_element_type=F32)


def fold_max(x):
    return jnp.max(x.reshape(GROUP // 8, 8, N), axis=0)


def fold_sum(x):
    return jnp.sum(x.reshape(GROUP // 8, 8, N), axis=0)


def spread_bias(last_frame, rel, table, window, strip_even, strip_odd):
    table[...] = jnp.zeros_like(table)
    for d in range(OFFSETS):
        for t in range(2 * FRAMES - 1):
            start = (t * OFFSETS + d) * OFFSETS
            table[d, :, 16 * t : 16 * t + OFFSETS] = rel[:, start : start + OFFSETS]
    for d in range(OFFSETS):
        for t in range(FRAMES):
            start = (FRAMES - 1 - t) * 16
            window[d, t] = table[d, :, start : start + 128]
    lane = lax.broadcasted_iota(jnp.int32, (8, 128), 1)
    col_j = lax.broadcasted_iota(jnp.int32, (8, 128), 0)
    frame_i = (lane % GROUP) // PADDED
    col_i = lane % PADDED
    index = jnp.maximum(frame_i * 16 + col_i - col_j + COLS - 1, 0)
    same_cols = jnp.logical_and((col_j < RS) == (col_i < RS), col_j < COLS)
    low = lane < GROUP

    def one_head(h, carry):
        for t in range(FRAMES):
            same = jnp.logical_and(
                same_cols,
                jnp.logical_or(jnp.logical_not(last_frame), (frame_i < FS) == (t < FS)),
            )
            got = []
            for d in range(OFFSETS):
                source = jnp.broadcast_to(window[d, t, pl.ds(h, 1), :], (8, 128))
                value = jnp.take_along_axis(source, index, axis=1)
                got.append(jnp.where(same, value, MASKED))
            for p in range(7):
                pair = jnp.where(low, got[2 * p], got[min(2 * p + 1, OFFSETS - 1)])
                strip_even[h, 8 * t : 8 * t + 8, 128 * p : 128 * p + 128] = pair
            for p in range(6):
                pair = jnp.where(low, got[2 * p + 1], got[2 * p + 2])
                strip_odd[h, 8 * t : 8 * t + 8, 128 * p : 128 * p + 128] = pair
        return carry

    lax.fori_loop(0, HEADS, one_head, 0)


def body(
    n_tm, n_height, tok, gain, w_qkv, w_proj, rel, cot, out, grad, part,
    x_in, c_in, x_out, c_out, x_rows, c_rows, standard, inverse,
    table, window, strip_even, strip_odd, w_t, k_rows, v_rows, qkv_t, q_masked, g_masked,
    ga_t, scores, exp_f, exp_b, norm, att_t, grad_t, pg, recv_a, send_b, recv_b, send_c, recv_c,
    local_sem, in_send, in_recv, out_send, out_recv,
    a_send, a_recv, b_send, b_recv, c_send, c_recv,
):
    n_y = n_tm // Z_SIZE
    a, b = lax.axis_index("tm"), lax.axis_index("height")
    y, z = a // Z_SIZE, a % Z_SIZE
    a_prev, a_next = (a + n_tm - 1) % n_tm, (a + 1) % n_tm
    b_prev, b_next = (b + n_height - 1) % n_height, (b + 1) % n_height

    def place(tm, height):
        return {"tm": tm, "height": height}

    def remote(src, dst, send, recv, tm, height):
        return pltpu.make_async_remote_copy(
            src_ref=src, dst_ref=dst, send_sem=send, recv_sem=recv,
            device_id=place(tm, height), device_id_type=MESH,
        )

    barrier = pltpu.get_barrier_semaphore()
    partners = [(a_prev, b), (a, b_prev), (a_prev, b_prev), (a_next, b), (a, b_next), (a_next, b_next)]
    partners += [(a, (b + d) % n_height) for d in range(1, n_height)]
    partners += [(y * Z_SIZE + (z + d) % Z_SIZE, b) for d in range(1, Z_SIZE)]
    partners += [(((y + d) % n_y) * Z_SIZE + z, b) for d in range(1, n_y)]
    for tm, height in partners:
        pl.semaphore_signal(barrier, inc=1, device_id=place(tm, height), device_id_type=MESH)
    pl.semaphore_wait(barrier, len(partners))

    def halo_in(src, dst, which):
        return [
            remote(src.at[0:FS, RS:ROWS], dst.at[FS:FRAMES, 0:KEEP], in_send.at[which, 0], in_recv.at[which, 0], a_prev, b),
            remote(src.at[FS:FRAMES, 0:RS], dst.at[0:FS, KEEP:ROWS], in_send.at[which, 1], in_recv.at[which, 1], a, b_prev),
            remote(src.at[0:FS, 0:RS], dst.at[FS:FRAMES, KEEP:ROWS], in_send.at[which, 2], in_recv.at[which, 2], a_prev, b_prev),
        ]

    def halo_out(src, dst, which):
        return [
            remote(src.at[FS:FRAMES, 0:KEEP], dst.at[0:FS, RS:ROWS], out_send.at[which, 0], out_recv.at[which, 0], a_next, b),
            remote(src.at[0:FS, KEEP:ROWS], dst.at[FS:FRAMES, 0:RS], out_send.at[which, 1], out_recv.at[which, 1], a, b_next),
            remote(src.at[FS:FRAMES, KEEP:ROWS], dst.at[0:FS, 0:RS], out_send.at[which, 2], out_recv.at[which, 2], a_next, b_next),
        ]

    x_copies = halo_in(tok, x_in, 0)
    c_copies = halo_in(cot, c_in, 1)
    x_own = pltpu.make_async_copy(tok.at[FS:FRAMES, RS:ROWS], x_in.at[0:FS, 0:KEEP], local_sem.at[0])
    c_own = pltpu.make_async_copy(cot.at[FS:FRAMES, RS:ROWS], c_in.at[0:FS, 0:KEEP], local_sem.at[1])
    for copy in x_copies + [x_own] + c_copies + [c_own]:
        copy.start()

    spread_bias(a == n_tm - 1, rel, table, window, strip_even, strip_odd)
    w_t[...] = w_qkv[...].T
    q_masked[...] = jnp.zeros_like(q_masked)
    g_masked[...] = jnp.zeros_like(g_masked)
    x_rows[...] = jnp.zeros_like(x_rows)
    c_rows[...] = jnp.zeros_like(c_rows)
    row_i = lax.broadcasted_iota(jnp.int32, (1, N), 1) // GROUP
    last_row = b == n_height - 1
    cap_low = jnp.where(jnp.logical_and(last_row, row_i >= KEEP), MASKED, 3e38)
    cap_high = jnp.where(jnp.logical_and(last_row, row_i < KEEP), MASKED, 3e38)
    scale = DIM ** (-0.5)

    for copy in x_copies:
        copy.wait_recv()
    x_own.wait()
    for r in range(ROWS):
        x_rows[r, :, 0:COLS, :] = x_in[:, r].astype(F32)
    x = x_rows[...].reshape(N, C)
    centred = x - jnp.mean(x, axis=-1, keepdims=True)
    inv = lax.rsqrt(jnp.mean(centred * centred, axis=-1, keepdims=True) + EPSILON)
    std = centred * inv
    standard[...] = std
    inverse[...] = inv
    normed = (std * gain[...]).astype(BF16)
    k_rows[...] = dot(normed, w_qkv[:, C : 2 * C]).astype(BF16)
    v_rows[...] = dot(normed, w_qkv[:, 2 * C :]).astype(BF16)
    q_t = (dot(w_t[0:C], normed, ((1,), (1,))) * scale).astype(BF16)
    qkv_t[0:C] = q_t
    qkv_t[C:] = dot(w_t[C:], normed, ((1,), (1,))).astype(BF16)
    for h in range(HEADS):
        q_masked[h, DIM * h : DIM * h + DIM] = q_t[DIM * h : DIM * h + DIM]

    def forward_head(h, carry):
        top = pl.multiple_of(h * DIM, DIM)
        scores[...] = dot(k_rows[...], q_masked[h])
        peak = None
        for r in range(ROWS):
            start = (ROWS - 1 - r) * GROUP
            if r % 2 == 0:
                bias = strip_even[h, :, start : start + N]
            else:
                bias = strip_odd[h, :, start - GROUP : start - GROUP + N]
            s = scores[GROUP * r : GROUP * r + GROUP] + bias
            s = jnp.minimum(s, cap_low if r < KEEP else cap_high)
            scores[GROUP * r : GROUP * r + GROUP] = s
            most = fold_max(s)
            peak = most if peak is None else jnp.maximum(peak, most)
        peak = jnp.max(peak, axis=0, keepdims=True)
        total = None
        for r in range(ROWS):
            e = jnp.exp(scores[GROUP * r : GROUP * r + GROUP] - peak)
            exp_f[h, GROUP * r : GROUP * r + GROUP] = e
            exp_b[h, GROUP * r : GROUP * r + GROUP] = e.astype(BF16)
            more = fold_sum(e)
            total = more if total is None else total + more
        over = 1.0 / jnp.sum(total, axis=0, keepdims=True)
        norm[h] = over
        v_t = qkv_t[pl.ds(2 * C + top, DIM)]
        att_t[pl.ds(top, DIM)] = (dot(v_t, exp_b[h]) * over).astype(BF16)
        return carry

    lax.fori_loop(0, HEADS, forward_head, 0)

    att = att_t[...].T
    y_out = (x_rows[...].reshape(N, C) + dot(att, w_proj[...])).reshape(ROWS, FRAMES, PADDED, C)
    for r in range(ROWS):
        x_out[:, r] = y_out[r, :, 0:COLS, :].astype(BF16)
    sent = halo_out(x_out, out, 0)
    sent_own = pltpu.make_async_copy(x_out.at[0:FS, 0:KEEP], out.at[FS:FRAMES, RS:ROWS], local_sem.at[2])
    for copy in sent:
        copy.start()
    sent_own.start()

    for copy in c_copies:
        copy.wait_recv()
    c_own.wait()
    for r in range(ROWS):
        c_rows[r, :, 0:COLS, :] = c_in[:, r].astype(F32)
    cot_b = c_rows[...].reshape(N, C).astype(BF16)
    width = C // n_height
    pg[...] = dot(att_t[...], cot_b).T.reshape(n_height, width, C)
    a_copies = []
    for d in range(1, n_height):
        peer = (b + d) % n_height
        copy = remote(pg.at[peer], recv_a.at[d], a_send.at[d], a_recv.at[d], a, peer)
        copy.start()
        a_copies.append(copy)
    ga_t[...] = dot(w_proj[...], cot_b, ((1,), (1,)))

    def backward_head(h, carry):
        top = pl.multiple_of(h * DIM, DIM)
        over = norm[h]
        ga = (ga_t[pl.ds(top, DIM)] * over).astype(BF16)
        g_masked[h, pl.ds(top, DIM)] = ga
        grad_t[pl.ds(2 * C + top, DIM)] = dot(ga, exp_b[h], ((1,), (1,))).astype(BF16)
        scores[...] = dot(v_rows[...], g_masked[h])
        total = None
        for r in range(ROWS):
            more = fold_sum(scores[GROUP * r : GROUP * r + GROUP] * exp_f[h, GROUP * r : GROUP * r + GROUP])
            total = more if total is None else total + more
        mean = jnp.sum(total, axis=0, keepdims=True) * over
        for r in range(ROWS):
            rows = slice(GROUP * r, GROUP * r + GROUP)
            exp_b[h, rows] = (exp_f[h, rows] * (scores[rows] - mean)).astype(BF16)
        ds = exp_b[h]
        k_t = qkv_t[pl.ds(C + top, DIM)]
        q_t = qkv_t[pl.ds(top, DIM)]
        grad_t[pl.ds(top, DIM)] = (dot(k_t, ds) * scale).astype(BF16)
        grad_t[pl.ds(C + top, DIM)] = dot(q_t, ds, ((1,), (1,))).astype(BF16)
        return carry

    lax.fori_loop(0, 3, backward_head, 0)

    for copy in a_copies:
        copy.wait_recv()
    held = pg[b]
    for d in range(1, n_height):
        held = held + recv_a[d]
    send_b[...] = held
    recv_b[z] = held
    b_copies, b_waits = [], []
    for d in range(1, Z_SIZE):
        peer, source = (z + d) % Z_SIZE, (z + Z_SIZE - d) % Z_SIZE
        copy = remote(send_b, recv_b.at[z], b_send.at[d], b_recv.at[d], y * Z_SIZE + peer, b)
        copy.start()
        b_copies.append(copy)
        b_waits.append(remote(send_b, recv_b.at[source], b_send.at[d], b_recv.at[d], y * Z_SIZE + peer, b))

    lax.fori_loop(3, 6, backward_head, 0)

    for copy in b_waits:
        copy.wait_recv()
    held = recv_b[0]
    for i in range(1, Z_SIZE):
        held = held + recv_b[i]
    send_c[...] = held
    recv_c[y] = held
    c_stage, c_waits = [], []
    for d in range(1, n_y):
        peer, source = (y + d) % n_y, (y + n_y - d) % n_y
        copy = remote(send_c, recv_c.at[y], c_send.at[d], c_recv.at[d], peer * Z_SIZE + z, b)
        copy.start()
        c_stage.append(copy)
        c_waits.append(remote(send_c, recv_c.at[source], c_send.at[d], c_recv.at[d], peer * Z_SIZE + z, b))

    lax.fori_loop(6, HEADS, backward_head, 0)

    g = dot(w_qkv[...], grad_t[...]).T * gain[...]
    std = standard[...]
    branch = inverse[...] * (
        g - jnp.mean(g, axis=-1, keepdims=True) - std * jnp.mean(g * std, axis=-1, keepdims=True)
    )
    back = (c_rows[...].reshape(N, C) + branch).reshape(ROWS, FRAMES, PADDED, C)
    for r in range(ROWS):
        c_out[:, r] = back[r, :, 0:COLS, :].astype(BF16)
    returned = halo_out(c_out, grad, 1)
    returned_own = pltpu.make_async_copy(c_out.at[0:FS, 0:KEEP], grad.at[FS:FRAMES, RS:ROWS], local_sem.at[3])
    for copy in returned:
        copy.start()
    returned_own.start()

    for copy in c_waits:
        copy.wait_recv()
    held = recv_c[0]
    for i in range(1, n_y):
        held = held + recv_c[i]
    tokens = n_tm * FRAMES * n_height * ROWS * COLS
    part[...] = held * (float(tokens) ** (-0.5))

    for copy in sent + returned:
        copy.wait_recv()
    sent_own.wait()
    returned_own.wait()
    for copy in x_copies + c_copies + sent + returned + a_copies + b_copies + c_stage:
        copy.wait_send()


def solution(mesh):
    n_tm, n_height = mesh.shape["tm"], mesh.shape["height"]
    n_y = n_tm // Z_SIZE
    width = C // n_height
    local = (FRAMES, ROWS, COLS, C)
    anywhere = pl.BlockSpec(memory_space=pl.ANY)
    vmem = pl.BlockSpec(memory_space=pltpu.VMEM)
    dma = pltpu.SemaphoreType.DMA
    V = pltpu.VMEM
    call = pl.pallas_call(
        functools.partial(body, n_tm, n_height),
        out_shape=(
            jax.ShapeDtypeStruct(local, BF16),
            jax.ShapeDtypeStruct(local, BF16),
            jax.ShapeDtypeStruct((width, C), F32),
        ),
        in_specs=[anywhere, vmem, vmem, vmem, vmem, anywhere],
        out_specs=(anywhere, anywhere, vmem),
        scratch_shapes=[
            V(local, BF16), V(local, BF16), V(local, BF16), V(local, BF16),
            V((ROWS, FRAMES, PADDED, C), F32), V((ROWS, FRAMES, PADDED, C), F32),
            V((N, C), F32), V((N, 1), F32),
            V((OFFSETS, HEADS, 256), F32), V((OFFSETS, FRAMES, HEADS, 128), F32),
            V((HEADS, GROUP, 896), F32), V((HEADS, GROUP, 768), F32),
            V((3 * C, C), BF16), V((N, C), BF16), V((N, C), BF16), V((3 * C, N), BF16),
            V((HEADS, C, N), BF16), V((HEADS, C, N), BF16),
            V((C, N), F32), V((N, N), F32), V((HEADS, N, N), F32), V((HEADS, N, N), BF16),
            V((HEADS, 1, N), F32), V((C, N), BF16), V((3 * C, N), BF16),
            V((n_height, width, C), F32), V((n_height, width, C), F32),
            V((width, C), F32), V((Z_SIZE, width, C), F32),
            V((width, C), F32), V((n_y, width, C), F32),
            dma((4,)), dma((2, 3)), dma((2, 3)), dma((2, 3)), dma((2, 3)),
            dma((n_height,)), dma((n_height,)), dma((Z_SIZE,)), dma((Z_SIZE,)), dma((n_y,)), dma((n_y,)),
        ],
        compiler_params=pltpu.CompilerParams(
            collective_id=0, has_side_effects=True, vmem_limit_bytes=56 * 1024 * 1024
        ),
        cost_estimate=pl.CostEstimate(flops=1_000_000_000, bytes_accessed=3_000_000, transcendentals=1_600_000),
    )

    def device(tokens, norm_gain, qkv_weight, proj_weight, rel_bias, cotangent):
        block_out, token_grad, proj_grad = call(
            tokens, norm_gain.reshape(1, C), qkv_weight, proj_weight, rel_bias, cotangent
        )
        return block_out, token_grad, proj_grad.T

    whole = P("tm", "height", None, None)
    return jax.shard_map(
        device,
        mesh=mesh,
        in_specs=(whole, P(), P(), P(), P(), whole),
        out_specs=(whole, whole, P(None, "height")),
        check_vma=False,
    )
```

```python
import functools

import jax
import jax.numpy as jnp
from jax import lax
from jax.experimental import pallas as pl
from jax.experimental.pallas import tpu as pltpu
from jax.sharding import PartitionSpec as P

HEADS = 8
DIM = 32
C = 256
FRAMES = 8
ROWS = 7
COLS = 7
SLABS = ROWS * COLS
N = SLABS * FRAMES
BAND = COLS * FRAMES
FS = FRAMES // 2
RS = ROWS // 2
KEEP = ROWS - RS
MAIN = KEEP * COLS
TAIL = RS * COLS
HALF = MAIN // 2
PART = (TAIL + 1) // 2
OFFSETS = 2 * ROWS - 1
CHUNKS = ((0, 112), (112, 224), (224, 336), (336, N))
Z_SIZE = 8
MASKED = -1e9
EPSILON = 1e-5
F32 = jnp.float32
BF16 = jnp.bfloat16
MESH = pl.DeviceIdType.MESH


def dot(a, b, dims=((1,), (0,))):
    return lax.dot_general(a, b, (dims, ((), ())), preferred_element_type=F32)


def fold_max(x):
    return jnp.max(x.reshape(x.shape[0] // 8, 8, N), axis=0)


def fold_sum(x):
    return jnp.sum(x.reshape(x.shape[0] // 8, 8, N), axis=0)


def late(shape):
    return lax.broadcasted_iota(jnp.int32, shape, 1) >= FS


def swap(x):
    return pltpu.roll(x, FS, 1)


def pack(main, tail, to_side, to_above, to_corner):
    first, second = main[0:HALF], main[HALF:MAIN]
    to_side[...] = jnp.where(late(first.shape), swap(second), first).astype(BF16)
    first, second = tail[0:PART], tail[TAIL - PART : TAIL]
    to_above[...] = jnp.where(late(first.shape), first, swap(second)).astype(BF16)
    to_corner[...] = jnp.where(late(first.shape), swap(second), first).astype(BF16)


def unpack(own, side, above, corner):
    own, side = own.astype(F32), side[...].astype(F32)
    above, corner = above[...].astype(F32), corner[...].astype(F32)
    mask = late(side.shape)
    yield 0, jnp.where(mask, own[0:HALF], side)
    yield HALF, jnp.where(mask, own[HALF:MAIN], swap(side))
    mask = late(above.shape)
    yield MAIN, jnp.where(mask, above, corner)
    last = jnp.where(mask, swap(above), swap(corner))
    yield MAIN + PART, last[2 * PART - TAIL :]


def spread_bias(last_frame, last_row, rel, table, rows_ahead, rows_behind, strip, bias):
    table[...] = jnp.zeros_like(table)
    for d in range(OFFSETS):
        for t in range(2 * FRAMES - 1):
            start = (t * OFFSETS + d) * OFFSETS
            table[d, :, 16 * t + 16 : 16 * t + 16 + OFFSETS] = rel[:, start : start + OFFSETS]
    lane = lax.broadcasted_iota(jnp.int32, (8, 128), 1)
    for tile in range(rows_ahead.shape[1]):
        place = (lane + 128 * tile) % BAND
        spot = (lane % FRAMES) * 16 + place // FRAMES
        first, last = 128 * tile // BAND, min((128 * tile + 127) // BAND, OFFSETS - 1)
        for c in range(COLS):
            same = (place < RS * FRAMES) == (c < RS)
            for side, rows in ((0, rows_behind), (128, rows_ahead)):
                value = None
                for d in range(first, last + 1):
                    piece = jnp.take_along_axis(table[d, :, side : side + 128], spot + (COLS - 1 - c), axis=1)
                    value = piece if value is None else jnp.where(lane >= BAND * d - 128 * tile, piece, value)
                rows[c, tile] = jnp.where(same, value, MASKED)
    frame_j = (lax.broadcasted_iota(jnp.int32, (8, 128), 0) + FS) % FRAMES
    frame_i = (lane + FS) % FRAMES
    index = (lane // FRAMES) * FRAMES + (frame_i - frame_j + FRAMES) % FRAMES
    forward = frame_i >= frame_j
    same_frames = jnp.logical_or(jnp.logical_not(last_frame), (frame_i < FS) == (frame_j < FS))
    row_i = lax.broadcasted_iota(jnp.int32, (1, N), 1) // BAND
    cap_low = jnp.where(jnp.logical_and(last_row, row_i >= KEEP), MASKED, 3e38)
    cap_high = jnp.where(jnp.logical_and(last_row, row_i < KEEP), MASKED, 3e38)

    def one_head(h, carry):
        for columns in ((0, 1, 2), (3, 4), (5, 6)):
            found = []
            for c in columns:
                for tile in range(strip.shape[1] // 128):
                    one = jnp.broadcast_to(rows_ahead[c, tile, pl.ds(h, 1), :], (8, 128))
                    two = jnp.broadcast_to(rows_behind[c, tile, pl.ds(h, 1), :], (8, 128))
                    one = jnp.take_along_axis(one, index, axis=1)
                    two = jnp.take_along_axis(two, index, axis=1)
                    found.append(jnp.where(same_frames, jnp.where(forward, one, two), MASKED))
            for n, value in enumerate(found):
                c, tile = columns[n // 6], n % 6
                strip[8 * c : 8 * c + 8, 128 * tile : 128 * tile + 128] = value
        for rows in ((0, 1, 2, 3), (4, 5, 6)):
            found = []
            for r in rows:
                start = (ROWS - 1 - r) * BAND
                found.append(jnp.minimum(strip[:, start : start + N], cap_low if r < KEEP else cap_high))
            for r, value in zip(rows, found):
                bias[h, BAND * r : BAND * r + BAND] = value
        return carry

    lax.fori_loop(0, HEADS, one_head, 0)


def body(
    n_tm, n_height, tok, gain, w_qkv, w_proj, rel, cot, out, grad, part,
    x_sent, c_sent, x_got, c_got, y_sent, g_sent, y_got, g_got, y_own, g_own, order, x_rows, c_rows, standard, inverse,
    table, rows_ahead, rows_behind, strip, bias, w_t, k_rows, v_rows, qkv_t, q_masked, g_masked,
    ga_t, scores, exp_f, exp_b, norm, att_t, grad_t, pg, got_core, held_core, got_z, held_z, got_xy, got_tm,
    in_send, in_recv, out_send, out_recv, core_send, core_recv,
    z_send, z_recv, xy_send, xy_recv, tm_send, tm_recv,
):
    n_xy = n_height // 2
    a, b = lax.axis_index("tm"), lax.axis_index("height")
    y, z = a // Z_SIZE, a % Z_SIZE
    xy, core = b // 2, b % 2
    a_prev, a_next = (a + n_tm - 1) % n_tm, (a + 1) % n_tm
    b_prev, b_next = (b + n_height - 1) % n_height, (b + 1) % n_height

    def place(tm, height):
        return {"tm": tm, "height": height}

    def remote(src, dst, send, recv, tm, height):
        return pltpu.make_async_remote_copy(
            src_ref=src, dst_ref=dst, send_sem=send, recv_sem=recv,
            device_id=place(tm, height), device_id_type=MESH,
        )

    barrier = pltpu.get_barrier_semaphore()
    stretch = pl.when(a < n_tm)
    partners = [(a_prev, b), (a, b_prev), (a_prev, b_prev), (a_next, b), (a, b_next), (a_next, b_next)]
    partners += [(a, xy * 2 + 1 - core)]
    partners += [(a, (xy + d) % n_xy * 2 + core) for d in range(1, n_xy)]
    partners += [((a + d) % n_tm, b) for d in range(1, n_tm)]
    for tm, height in partners:
        pl.semaphore_signal(barrier, inc=1, device_id=place(tm, height), device_id_type=MESH)
    pack(tok[TAIL:].astype(F32), tok[0:TAIL].astype(F32), *x_sent)
    pl.semaphore_wait(barrier, len(partners))

    def halo(src, dst, send, recv, tm, height):
        return [
            remote(src[0], dst[0], send.at[0], recv.at[0], tm, b),
            remote(src[1], dst[1], send.at[1], recv.at[1], a, height),
            remote(src[2], dst[2], send.at[2], recv.at[2], tm, height),
        ]

    x_copies = halo(x_sent, x_got, in_send.at[0], in_recv.at[0], a_prev, b_prev)
    c_copies = halo(c_sent, c_got, in_send.at[1], in_recv.at[1], a_prev, b_prev)
    for copy in x_copies:
        copy.start()

    scale = DIM ** (-0.5)

    @stretch
    def alone():
        pack(cot[TAIL:].astype(F32), cot[0:TAIL].astype(F32), *c_sent)
        spread_bias(
            a == n_tm - 1, b == n_height - 1, rel, table, rows_ahead, rows_behind, strip, bias
        )
        w_t[...] = w_qkv[...].T
        q_masked[...] = jnp.zeros_like(q_masked)
        g_masked[...] = jnp.zeros_like(g_masked)
        column = lax.broadcasted_iota(jnp.int32, (C, C), 1)
        e, q = column % 2, column // 2 % n_xy
        z_of, core_of = column // (2 * n_xy) % Z_SIZE, column // (2 * n_xy * Z_SIZE)
        channel = (q * 2 + core_of) * (2 * Z_SIZE) + z_of * 2 + e
        order[...] = (lax.broadcasted_iota(jnp.int32, (C, C), 0) == channel).astype(BF16)

    for copy in x_copies:
        copy.wait_recv()
    for copy in c_copies:
        copy.start()
    @stretch
    def forward():
        for at, value in unpack(tok[TAIL:], *x_got):
            x_rows[at : at + value.shape[0]] = value
        x = x_rows[...].reshape(N, C)
        centred = x - jnp.mean(x, axis=-1, keepdims=True)
        inv = lax.rsqrt(jnp.mean(centred * centred, axis=-1, keepdims=True) + EPSILON)
        std = centred * inv
        standard[...] = std
        inverse[...] = inv
        normed = (std * gain[...]).astype(BF16)
        k_rows[...] = dot(normed, w_qkv[:, C : 2 * C]).astype(BF16)
        v_rows[...] = dot(normed, w_qkv[:, 2 * C :]).astype(BF16)
        q_t = (dot(w_t[0:C], normed, ((1,), (1,))) * scale).astype(BF16)
        qkv_t[0:C] = q_t
        qkv_t[C:] = dot(w_t[C:], normed, ((1,), (1,))).astype(BF16)
        for h in range(HEADS):
            q_masked[h, DIM * h : DIM * h + DIM] = q_t[DIM * h : DIM * h + DIM]

        def forward_head(h, carry):
            top = pl.multiple_of(h * DIM, DIM)
            scores[...] = dot(k_rows[...], q_masked[h])
            peak = None
            for lo, hi in CHUNKS:
                s = scores[lo:hi] + bias[h, lo:hi]
                scores[lo:hi] = s
                most = fold_max(s)
                peak = most if peak is None else jnp.maximum(peak, most)
            peak = jnp.max(peak, axis=0, keepdims=True)
            total = None
            for lo, hi in CHUNKS:
                e = jnp.exp(scores[lo:hi] - peak)
                exp_f[h, lo:hi] = e
                exp_b[h, lo:hi] = e.astype(BF16)
                more = fold_sum(e)
                total = more if total is None else total + more
            over = 1.0 / jnp.sum(total, axis=0, keepdims=True)
            norm[h] = over
            v_t = qkv_t[pl.ds(2 * C + top, DIM)]
            att_t[pl.ds(top, DIM)] = (dot(v_t, exp_b[h]) * over).astype(BF16)
            return carry

        lax.fori_loop(0, HEADS, forward_head, 0)

        att = att_t[...].T
        y_out = (x_rows[...].reshape(N, C) + dot(att, w_proj[...])).reshape(SLABS, FRAMES, C)
        pack(y_out[0:MAIN], y_out[MAIN:], *y_sent)
        y_own[...] = y_out[0:MAIN].astype(BF16)

    sent = halo(y_sent, y_got, out_send.at[0], out_recv.at[0], a_next, b_next)
    for copy in sent:
        copy.start()

    for copy in c_copies:
        copy.wait_recv()
    @stretch
    def partial_gradient():
        for at, value in unpack(cot[TAIL:], *c_got):
            c_rows[at : at + value.shape[0]] = value
        cot_b = c_rows[...].reshape(N, C).astype(BF16)
        cot_order = dot(cot_b, order[...]).astype(BF16)
        pg[...] = dot(att_t[...], cot_order).T.reshape(2, Z_SIZE, 2 * n_xy, C)

    to_core = remote(pg.at[1 - core], got_core, core_send.at[0], core_recv.at[0], a, xy * 2 + 1 - core)
    to_core.start()

    def backward_head(h, carry):
        top = pl.multiple_of(h * DIM, DIM)
        over = norm[h]
        ga = (ga_t[pl.ds(top, DIM)] * over).astype(BF16)
        g_masked[h, pl.ds(top, DIM)] = ga
        grad_t[pl.ds(2 * C + top, DIM)] = dot(ga, exp_b[h], ((1,), (1,))).astype(BF16)
        scores[...] = dot(v_rows[...], g_masked[h])
        total = None
        for lo, hi in CHUNKS:
            more = fold_sum(scores[lo:hi] * exp_f[h, lo:hi])
            total = more if total is None else total + more
        mean = jnp.sum(total, axis=0, keepdims=True) * over
        for lo, hi in CHUNKS:
            exp_b[h, lo:hi] = (exp_f[h, lo:hi] * (scores[lo:hi] - mean)).astype(BF16)
        ds = exp_b[h]
        k_t = qkv_t[pl.ds(C + top, DIM)]
        q_t = qkv_t[pl.ds(top, DIM)]
        grad_t[pl.ds(top, DIM)] = (dot(k_t, ds) * scale).astype(BF16)
        grad_t[pl.ds(C + top, DIM)] = dot(q_t, ds, ((1,), (1,))).astype(BF16)
        return carry

    @stretch
    def backward_first():
        cot_b = c_rows[...].reshape(N, C).astype(BF16)
        ga_t[...] = dot(w_proj[...], cot_b, ((1,), (1,)))
        lax.fori_loop(0, 2, backward_head, 0)

    to_core.wait_recv()
    held_core[...] = pg[core] + got_core[...]
    z_copies = []
    for d in range(1, Z_SIZE):
        peer = (z + d) % Z_SIZE
        copy = remote(held_core.at[peer], got_z.at[d], z_send.at[d], z_recv.at[d], y * Z_SIZE + peer, b)
        copy.start()
        z_copies.append(copy)

    @stretch
    def backward_second():
        lax.fori_loop(2, 5, backward_head, 0)

    for copy in z_copies:
        copy.wait_recv()
    held = held_core[z]
    for d in range(1, Z_SIZE):
        held = held + got_z[d]
    for i in range(n_xy):
        held_z[i, 0:2] = held[2 * i : 2 * i + 2, 0:128]
        held_z[i, 2:4] = held[2 * i : 2 * i + 2, 128:256]
    xy_copies = []
    for d in range(1, n_xy):
        peer = (xy + d) % n_xy
        copy = remote(held_z.at[peer], got_xy.at[d], xy_send.at[d], xy_recv.at[d], a, peer * 2 + core)
        copy.start()
        xy_copies.append(copy)

    @stretch
    def backward_third():
        lax.fori_loop(5, HEADS, backward_head, 0)

    for copy in xy_copies:
        copy.wait_recv()
    held = held_z[xy]
    for d in range(1, n_xy):
        held = held + got_xy[d]
    got_tm[a] = held
    tm_copies, tm_waits = [], []
    for d in range(1, n_tm):
        peer, source = (a + d) % n_tm, (a + n_tm - d) % n_tm
        copy = remote(got_tm.at[a], got_tm.at[a], tm_send.at[d], tm_recv.at[d], peer, b)
        copy.start()
        tm_copies.append(copy)
        tm_waits.append(remote(got_tm.at[a], got_tm.at[source], tm_send.at[d], tm_recv.at[d], peer, b))

    @stretch
    def backward_rest():
        g = dot(w_qkv[...], grad_t[...]).T * gain[...]
        std = standard[...]
        branch = inverse[...] * (
            g - jnp.mean(g, axis=-1, keepdims=True) - std * jnp.mean(g * std, axis=-1, keepdims=True)
        )
        back = (c_rows[...].reshape(N, C) + branch).reshape(SLABS, FRAMES, C)
        pack(back[0:MAIN], back[MAIN:], *g_sent)
        g_own[...] = back[0:MAIN].astype(BF16)

    returned = halo(g_sent, g_got, out_send.at[1], out_recv.at[1], a_next, b_next)
    for copy in returned:
        copy.start()

    def finish(result, own, got):
        for at, value in unpack(own, *got):
            at = (at + TAIL) % SLABS
            result[at : at + value.shape[0]] = value.astype(BF16)

    for copy in sent:
        copy.wait_recv()
    finish(out, y_own[...], y_got)
    for copy in tm_waits:
        copy.wait_recv()
    tokens = n_tm * FRAMES * n_height * ROWS * COLS
    for i in range(Z_SIZE):
        held = got_tm[i]
        for j in range(1, n_tm // Z_SIZE):
            held = held + got_tm[j * Z_SIZE + i]
        held = held * (float(tokens) ** (-0.5))
        part[2 * i : 2 * i + 2, 0:128] = held[0:2]
        part[2 * i : 2 * i + 2, 128:256] = held[2:4]

    for copy in returned:
        copy.wait_recv()
    finish(grad, g_own[...], g_got)
    for copy in x_copies + c_copies + sent + returned + [to_core] + z_copies + xy_copies + tm_copies:
        copy.wait_send()


def solution(mesh):
    n_tm, n_height = mesh.shape["tm"], mesh.shape["height"]
    n_xy = n_height // 2
    width = C // n_height
    local = (SLABS, FRAMES, C)
    vmem = pl.BlockSpec(memory_space=pltpu.VMEM)
    dma = pltpu.SemaphoreType.DMA
    V = pltpu.VMEM
    call = pl.pallas_call(
        functools.partial(body, n_tm, n_height),
        out_shape=(
            jax.ShapeDtypeStruct(local, BF16),
            jax.ShapeDtypeStruct(local, BF16),
            jax.ShapeDtypeStruct((width, C), F32),
        ),
        in_specs=[vmem] * 6,
        out_specs=(vmem, vmem, vmem),
        scratch_shapes=[
            *[[V((n, FRAMES, C), BF16) for n in (HALF, PART, PART)] for _ in range(8)],
            V((MAIN, FRAMES, C), BF16), V((MAIN, FRAMES, C), BF16), V((C, C), BF16), V(local, F32), V(local, F32), V((N, C), F32), V((N, 1), F32),
            V((OFFSETS, HEADS, 256), F32),
            V((COLS, 6, HEADS, 128), F32), V((COLS, 6, HEADS, 128), F32), V((BAND, 768), F32), V((HEADS, N, N), F32),
            V((3 * C, C), BF16), V((N, C), BF16), V((N, C), BF16), V((3 * C, N), BF16),
            V((HEADS, C, N), BF16), V((HEADS, C, N), BF16),
            V((C, N), F32), V((N, N), F32), V((HEADS, N, N), F32), V((HEADS, N, N), BF16),
            V((HEADS, 1, N), F32), V((C, N), BF16), V((3 * C, N), BF16),
            V((2, Z_SIZE, 2 * n_xy, C), F32), V((Z_SIZE, 2 * n_xy, C), F32), V((Z_SIZE, 2 * n_xy, C), F32),
            V((Z_SIZE, 2 * n_xy, C), F32), V((n_xy, 4, 128), F32), V((n_xy, 4, 128), F32), V((n_tm, 4, 128), F32),
            dma((2, 3)), dma((2, 3)), dma((2, 3)), dma((2, 3)),
            dma((1,)), dma((1,)), dma((Z_SIZE,)), dma((Z_SIZE,)),
            dma((n_xy,)), dma((n_xy,)), dma((n_tm,)), dma((n_tm,)),
        ],
        compiler_params=pltpu.CompilerParams(
            collective_id=0, has_side_effects=True, vmem_limit_bytes=56 * 1024 * 1024
        ),
        cost_estimate=pl.CostEstimate(flops=1_000_000_000, bytes_accessed=3_000_000, transcendentals=1_600_000),
    )

    def device(tokens, norm_gain, qkv_weight, proj_weight, rel_bias, cotangent):
        def inside(grid):
            return grid.transpose(1, 2, 0, 3).reshape(local)

        def outside(slabs):
            return slabs.reshape(ROWS, COLS, FRAMES, C).transpose(2, 0, 1, 3)

        block_out, token_grad, proj_grad = call(
            inside(tokens), norm_gain.reshape(1, C), qkv_weight, proj_weight, rel_bias, inside(cotangent)
        )
        return outside(block_out), outside(token_grad), proj_grad.T

    whole = P("tm", "height", None, None)
    return jax.shard_map(
        device,
        mesh=mesh,
        in_specs=(whole, P(), P(), P(), P(), whole),
        out_specs=(whole, whole, P(None, "height")),
        check_vma=False,
    )
```

```python
import functools

import jax
import jax.numpy as jnp
from jax import lax
from jax.experimental import pallas as pl
from jax.experimental.pallas import tpu as pltpu
from jax.sharding import PartitionSpec as P

HEADS = 8
DIM = 32
C = 256
FRAMES = 8
ROWS = 7
COLS = 7
SLABS = ROWS * COLS
N = SLABS * FRAMES
BAND = COLS * FRAMES
FS = FRAMES // 2
RS = ROWS // 2
KEEP = ROWS - RS
MAIN = KEEP * COLS
TAIL = RS * COLS
HALF = MAIN // 2
PART = (TAIL + 1) // 2
OFFSETS = 2 * ROWS - 1
CHUNKS = ((0, 112), (112, 224), (224, 336), (336, N))
Z_SIZE = 8
MASKED = -1e9
EPSILON = 1e-5
F32 = jnp.float32
BF16 = jnp.bfloat16
MESH = pl.DeviceIdType.MESH


def dot(a, b, dims=((1,), (0,))):
    return lax.dot_general(a, b, (dims, ((), ())), preferred_element_type=F32)


def fold_max(x):
    return jnp.max(x.reshape(x.shape[0] // 8, 8, N), axis=0)


def fold_sum(x):
    return jnp.sum(x.reshape(x.shape[0] // 8, 8, N), axis=0)


def late(shape):
    return lax.broadcasted_iota(jnp.int32, shape, 1) >= FS


def swap(x):
    return pltpu.roll(x, FS, 1)


def pack(main, tail, to_side, to_above, to_corner):
    first, second = main[0:HALF], main[HALF:MAIN]
    to_side[...] = jnp.where(late(first.shape), swap(second), first).astype(BF16)
    first, second = tail[0:PART], tail[TAIL - PART : TAIL]
    to_above[...] = jnp.where(late(first.shape), first, swap(second)).astype(BF16)
    to_corner[...] = jnp.where(late(first.shape), swap(second), first).astype(BF16)


def unpack(own, side, above, corner):
    own, side = own.astype(F32), side[...].astype(F32)
    above, corner = above[...].astype(F32), corner[...].astype(F32)
    mask = late(side.shape)
    yield 0, jnp.where(mask, own[0:HALF], side)
    yield HALF, jnp.where(mask, own[HALF:MAIN], swap(side))
    mask = late(above.shape)
    yield MAIN, jnp.where(mask, above, corner)
    last = jnp.where(mask, swap(above), swap(corner))
    yield MAIN + PART, last[2 * PART - TAIL :]


def spread_bias(last_frame, last_row, rel, table, rows_ahead, rows_behind, strip, bias):
    table[...] = jnp.zeros_like(table)
    for d in range(OFFSETS):
        for t in range(2 * FRAMES - 1):
            start = (t * OFFSETS + d) * OFFSETS
            table[d, :, 16 * t + 16 : 16 * t + 16 + OFFSETS] = rel[:, start : start + OFFSETS]
    lane = lax.broadcasted_iota(jnp.int32, (8, 128), 1)
    for tile in range(rows_ahead.shape[1]):
        place = (lane + 128 * tile) % BAND
        spot = (lane % FRAMES) * 16 + place // FRAMES
        first, last = 128 * tile // BAND, min((128 * tile + 127) // BAND, OFFSETS - 1)
        for c in range(COLS):
            same = (place < RS * FRAMES) == (c < RS)
            for side, rows in ((0, rows_behind), (128, rows_ahead)):
                value = None
                for d in range(first, last + 1):
                    piece = jnp.take_along_axis(table[d, :, side : side + 128], spot + (COLS - 1 - c), axis=1)
                    value = piece if value is None else jnp.where(lane >= BAND * d - 128 * tile, piece, value)
                rows[c, tile] = jnp.where(same, value, MASKED)
    frame_j = (lax.broadcasted_iota(jnp.int32, (8, 128), 0) + FS) % FRAMES
    frame_i = (lane + FS) % FRAMES
    index = (lane // FRAMES) * FRAMES + (frame_i - frame_j + FRAMES) % FRAMES
    forward = frame_i >= frame_j
    same_frames = jnp.logical_or(jnp.logical_not(last_frame), (frame_i < FS) == (frame_j < FS))
    row_i = lax.broadcasted_iota(jnp.int32, (1, N), 1) // BAND
    cap_low = jnp.where(jnp.logical_and(last_row, row_i >= KEEP), MASKED, 3e38)
    cap_high = jnp.where(jnp.logical_and(last_row, row_i < KEEP), MASKED, 3e38)

    def one_head(h, carry):
        for columns in ((0, 1, 2), (3, 4), (5, 6)):
            found = []
            for c in columns:
                for tile in range(strip.shape[1] // 128):
                    one = jnp.broadcast_to(rows_ahead[c, tile, pl.ds(h, 1), :], (8, 128))
                    two = jnp.broadcast_to(rows_behind[c, tile, pl.ds(h, 1), :], (8, 128))
                    one = jnp.take_along_axis(one, index, axis=1)
                    two = jnp.take_along_axis(two, index, axis=1)
                    found.append(jnp.where(same_frames, jnp.where(forward, one, two), MASKED))
            for n, value in enumerate(found):
                c, tile = columns[n // 6], n % 6
                strip[8 * c : 8 * c + 8, 128 * tile : 128 * tile + 128] = value
        for rows in ((0, 1, 2, 3), (4, 5, 6)):
            found = []
            for r in rows:
                start = (ROWS - 1 - r) * BAND
                found.append(jnp.minimum(strip[:, start : start + N], cap_low if r < KEEP else cap_high))
            for r, value in zip(rows, found):
                bias[h, BAND * r : BAND * r + BAND] = value
        return carry

    lax.fori_loop(0, HEADS, one_head, 0)


def body(
    n_tm, n_height, tok, gain, w_qkv, w_proj, rel, cot, out, grad, part,
    x_sent, c_sent, x_got, c_got, y_sent, g_sent, y_got, g_got, y_own, g_own, order, x_rows, c_rows, standard, inverse,
    table, rows_ahead, rows_behind, strip, bias, w_t, k_rows, v_rows, qkv_t, q_masked, g_masked,
    ga_t, scores, exp_f, exp_b, norm, att_t, grad_t, pg, got_core, held_core, got_z, held_z, got_xy, got_tm,
    in_send, in_recv, out_send, out_recv, core_send, core_recv,
    z_send, z_recv, xy_send, xy_recv, tm_send, tm_recv,
):
    n_xy = n_height // 2
    a, b = lax.axis_index("tm"), lax.axis_index("height")
    y, z = a // Z_SIZE, a % Z_SIZE
    xy, core = b // 2, b % 2
    a_prev, a_next = (a + n_tm - 1) % n_tm, (a + 1) % n_tm
    b_prev, b_next = (b + n_height - 1) % n_height, (b + 1) % n_height

    def place(tm, height):
        return {"tm": tm, "height": height}

    def remote(src, dst, send, recv, tm, height):
        return pltpu.make_async_remote_copy(
            src_ref=src, dst_ref=dst, send_sem=send, recv_sem=recv,
            device_id=place(tm, height), device_id_type=MESH,
        )

    barrier = pltpu.get_barrier_semaphore()
    stretch = pl.when(a < n_tm)
    partners = [(a_prev, b), (a, b_prev), (a_prev, b_prev), (a_next, b), (a, b_next), (a_next, b_next)]
    partners += [(a, xy * 2 + 1 - core)]
    partners += [(a, (xy + d) % n_xy * 2 + core) for d in range(1, n_xy)]
    partners += [((a + d) % n_tm, b) for d in range(1, n_tm)]
    for tm, height in partners:
        pl.semaphore_signal(barrier, inc=1, device_id=place(tm, height), device_id_type=MESH)
    pack(tok[TAIL:].astype(F32), tok[0:TAIL].astype(F32), *x_sent)
    pl.semaphore_wait(barrier, len(partners))

    def halo(src, dst, send, recv, tm, height):
        return [
            remote(src[0], dst[0], send.at[0], recv.at[0], tm, b),
            remote(src[1], dst[1], send.at[1], recv.at[1], a, height),
            remote(src[2], dst[2], send.at[2], recv.at[2], tm, height),
        ]

    x_copies = halo(x_sent, x_got, in_send.at[0], in_recv.at[0], a_prev, b_prev)
    c_copies = halo(c_sent, c_got, in_send.at[1], in_recv.at[1], a_prev, b_prev)
    for copy in x_copies:
        copy.start()

    scale = DIM ** (-0.5)

    @stretch
    def alone():
        pack(cot[TAIL:].astype(F32), cot[0:TAIL].astype(F32), *c_sent)
        spread_bias(
            a == n_tm - 1, b == n_height - 1, rel, table, rows_ahead, rows_behind, strip, bias
        )
        w_t[...] = w_qkv[...].T
        q_masked[...] = jnp.zeros_like(q_masked)
        g_masked[...] = jnp.zeros_like(g_masked)
        column = lax.broadcasted_iota(jnp.int32, (C, C), 1)
        e, q = column % 2, column // 2 % n_xy
        z_of, core_of = column // (2 * n_xy) % Z_SIZE, column // (2 * n_xy * Z_SIZE)
        channel = (q * 2 + core_of) * (2 * Z_SIZE) + z_of * 2 + e
        order[...] = (lax.broadcasted_iota(jnp.int32, (C, C), 0) == channel).astype(BF16)

    for copy in x_copies:
        copy.wait_recv()
    for copy in c_copies:
        copy.start()
    @stretch
    def forward():
        for at, value in unpack(tok[TAIL:], *x_got):
            x_rows[at : at + value.shape[0]] = value
        x = x_rows[...].reshape(N, C)
        centred = x - jnp.mean(x, axis=-1, keepdims=True)
        inv = lax.rsqrt(jnp.mean(centred * centred, axis=-1, keepdims=True) + EPSILON)
        std = centred * inv
        standard[...] = std
        inverse[...] = inv
        normed = (std * gain[...]).astype(BF16)
        k_rows[...] = dot(normed, w_qkv[:, C : 2 * C]).astype(BF16)
        v_rows[...] = dot(normed, w_qkv[:, 2 * C :]).astype(BF16)
        q_t = (dot(w_t[0:C], normed, ((1,), (1,))) * scale).astype(BF16)
        qkv_t[0:C] = q_t
        qkv_t[C:] = dot(w_t[C:], normed, ((1,), (1,))).astype(BF16)
        for h in range(HEADS):
            q_masked[h, DIM * h : DIM * h + DIM] = q_t[DIM * h : DIM * h + DIM]

        def forward_head(h, carry):
            top = pl.multiple_of(h * DIM, DIM)
            scores[...] = dot(k_rows[...], q_masked[h])
            peak = None
            for lo, hi in CHUNKS:
                s = scores[lo:hi] + bias[h, lo:hi]
                scores[lo:hi] = s
                most = fold_max(s)
                peak = most if peak is None else jnp.maximum(peak, most)
            peak = jnp.max(peak, axis=0, keepdims=True)
            total = None
            for lo, hi in CHUNKS:
                e = jnp.exp(scores[lo:hi] - peak)
                exp_f[h, lo:hi] = e
                exp_b[h, lo:hi] = e.astype(BF16)
                more = fold_sum(e)
                total = more if total is None else total + more
            over = 1.0 / jnp.sum(total, axis=0, keepdims=True)
            norm[h] = over
            v_t = qkv_t[pl.ds(2 * C + top, DIM)]
            att_t[pl.ds(top, DIM)] = (dot(v_t, exp_b[h]) * over).astype(BF16)
            return carry

        def forward_pair(i, carry):
            return forward_head(2 * i + 1, forward_head(2 * i, carry))

        lax.fori_loop(0, HEADS // 2, forward_pair, 0)

        att = att_t[...].T
        y_out = (x_rows[...].reshape(N, C) + dot(att, w_proj[...])).reshape(SLABS, FRAMES, C)
        pack(y_out[0:MAIN], y_out[MAIN:], *y_sent)
        y_own[...] = y_out[0:MAIN].astype(BF16)

    sent = halo(y_sent, y_got, out_send.at[0], out_recv.at[0], a_next, b_next)
    for copy in sent:
        copy.start()

    for copy in c_copies:
        copy.wait_recv()
    @stretch
    def partial_gradient():
        for at, value in unpack(cot[TAIL:], *c_got):
            c_rows[at : at + value.shape[0]] = value
        cot_b = c_rows[...].reshape(N, C).astype(BF16)
        cot_order = dot(cot_b, order[...]).astype(BF16)
        pg[...] = dot(att_t[...], cot_order).T.reshape(2, Z_SIZE, 2 * n_xy, C)

    to_core = remote(pg.at[1 - core], got_core, core_send.at[0], core_recv.at[0], a, xy * 2 + 1 - core)
    to_core.start()

    def backward_head(h, carry):
        top = pl.multiple_of(h * DIM, DIM)
        over = norm[h]
        ga = (ga_t[pl.ds(top, DIM)] * over).astype(BF16)
        g_masked[h, pl.ds(top, DIM)] = ga
        grad_t[pl.ds(2 * C + top, DIM)] = dot(ga, exp_b[h], ((1,), (1,))).astype(BF16)
        scores[...] = dot(v_rows[...], g_masked[h])
        total = None
        for lo, hi in CHUNKS:
            more = fold_sum(scores[lo:hi] * exp_f[h, lo:hi])
            total = more if total is None else total + more
        mean = jnp.sum(total, axis=0, keepdims=True) * over
        for lo, hi in CHUNKS:
            exp_b[h, lo:hi] = (exp_f[h, lo:hi] * (scores[lo:hi] - mean)).astype(BF16)
        ds = exp_b[h]
        k_t = qkv_t[pl.ds(C + top, DIM)]
        q_t = qkv_t[pl.ds(top, DIM)]
        grad_t[pl.ds(top, DIM)] = (dot(k_t, ds) * scale).astype(BF16)
        grad_t[pl.ds(C + top, DIM)] = dot(q_t, ds, ((1,), (1,))).astype(BF16)
        return carry

    @stretch
    def backward_first():
        cot_b = c_rows[...].reshape(N, C).astype(BF16)
        ga_t[...] = dot(w_proj[...], cot_b, ((1,), (1,)))
        lax.fori_loop(0, 2, backward_head, 0)

    to_core.wait_recv()
    held_core[...] = pg[core] + got_core[...]
    z_copies = []
    for d in range(1, Z_SIZE):
        peer = (z + d) % Z_SIZE
        copy = remote(held_core.at[peer], got_z.at[d], z_send.at[d], z_recv.at[d], y * Z_SIZE + peer, b)
        copy.start()
        z_copies.append(copy)

    @stretch
    def backward_second():
        lax.fori_loop(2, 5, backward_head, 0)

    for copy in z_copies:
        copy.wait_recv()
    held = held_core[z]
    for d in range(1, Z_SIZE):
        held = held + got_z[d]
    for i in range(n_xy):
        held_z[i, 0:2] = held[2 * i : 2 * i + 2, 0:128]
        held_z[i, 2:4] = held[2 * i : 2 * i + 2, 128:256]
    xy_copies = []
    for d in range(1, n_xy):
        peer = (xy + d) % n_xy
        copy = remote(held_z.at[peer], got_xy.at[d], xy_send.at[d], xy_recv.at[d], a, peer * 2 + core)
        copy.start()
        xy_copies.append(copy)

    @stretch
    def backward_third():
        lax.fori_loop(5, HEADS, backward_head, 0)

    @stretch
    def backward_rest():
        g = dot(w_qkv[...], grad_t[...]).T * gain[...]
        std = standard[...]
        branch = inverse[...] * (
            g - jnp.mean(g, axis=-1, keepdims=True) - std * jnp.mean(g * std, axis=-1, keepdims=True)
        )
        back = (c_rows[...].reshape(N, C) + branch).reshape(SLABS, FRAMES, C)
        pack(back[0:MAIN], back[MAIN:], *g_sent)
        g_own[...] = back[0:MAIN].astype(BF16)

    returned = halo(g_sent, g_got, out_send.at[1], out_recv.at[1], a_next, b_next)
    for copy in returned:
        copy.start()

    for copy in xy_copies:
        copy.wait_recv()
    held = held_z[xy]
    for d in range(1, n_xy):
        held = held + got_xy[d]
    got_tm[a] = held
    tm_copies, tm_waits = [], []
    for d in range(1, n_tm):
        peer, source = (a + d) % n_tm, (a + n_tm - d) % n_tm
        copy = remote(got_tm.at[a], got_tm.at[a], tm_send.at[d], tm_recv.at[d], peer, b)
        copy.start()
        tm_copies.append(copy)
        tm_waits.append(remote(got_tm.at[a], got_tm.at[source], tm_send.at[d], tm_recv.at[d], peer, b))

    def finish(result, own, got):
        for at, value in unpack(own, *got):
            at = (at + TAIL) % SLABS
            result[at : at + value.shape[0]] = value.astype(BF16)

    for copy in sent:
        copy.wait_recv()
    finish(out, y_own[...], y_got)
    for copy in tm_waits:
        copy.wait_recv()
    tokens = n_tm * FRAMES * n_height * ROWS * COLS
    for i in range(Z_SIZE):
        held = got_tm[i]
        for j in range(1, n_tm // Z_SIZE):
            held = held + got_tm[j * Z_SIZE + i]
        held = held * (float(tokens) ** (-0.5))
        part[2 * i : 2 * i + 2, 0:128] = held[0:2]
        part[2 * i : 2 * i + 2, 128:256] = held[2:4]

    for copy in returned:
        copy.wait_recv()
    finish(grad, g_own[...], g_got)
    for copy in x_copies + c_copies + sent + returned + [to_core] + z_copies + xy_copies + tm_copies:
        copy.wait_send()


def solution(mesh):
    n_tm, n_height = mesh.shape["tm"], mesh.shape["height"]
    n_xy = n_height // 2
    width = C // n_height
    local = (SLABS, FRAMES, C)
    vmem = pl.BlockSpec(memory_space=pltpu.VMEM)
    dma = pltpu.SemaphoreType.DMA
    V = pltpu.VMEM
    call = pl.pallas_call(
        functools.partial(body, n_tm, n_height),
        out_shape=(
            jax.ShapeDtypeStruct(local, BF16),
            jax.ShapeDtypeStruct(local, BF16),
            jax.ShapeDtypeStruct((width, C), F32),
        ),
        in_specs=[vmem] * 6,
        out_specs=(vmem, vmem, vmem),
        scratch_shapes=[
            *[[V((n, FRAMES, C), BF16) for n in (HALF, PART, PART)] for _ in range(8)],
            V((MAIN, FRAMES, C), BF16), V((MAIN, FRAMES, C), BF16), V((C, C), BF16), V(local, F32), V(local, F32), V((N, C), F32), V((N, 1), F32),
            V((OFFSETS, HEADS, 256), F32),
            V((COLS, 6, HEADS, 128), F32), V((COLS, 6, HEADS, 128), F32), V((BAND, 768), F32), V((HEADS, N, N), F32),
            V((3 * C, C), BF16), V((N, C), BF16), V((N, C), BF16), V((3 * C, N), BF16),
            V((HEADS, C, N), BF16), V((HEADS, C, N), BF16),
            V((C, N), F32), V((N, N), F32), V((HEADS, N, N), F32), V((HEADS, N, N), BF16),
            V((HEADS, 1, N), F32), V((C, N), BF16), V((3 * C, N), BF16),
            V((2, Z_SIZE, 2 * n_xy, C), F32), V((Z_SIZE, 2 * n_xy, C), F32), V((Z_SIZE, 2 * n_xy, C), F32),
            V((Z_SIZE, 2 * n_xy, C), F32), V((n_xy, 4, 128), F32), V((n_xy, 4, 128), F32), V((n_tm, 4, 128), F32),
            dma((2, 3)), dma((2, 3)), dma((2, 3)), dma((2, 3)),
            dma((1,)), dma((1,)), dma((Z_SIZE,)), dma((Z_SIZE,)),
            dma((n_xy,)), dma((n_xy,)), dma((n_tm,)), dma((n_tm,)),
        ],
        compiler_params=pltpu.CompilerParams(
            collective_id=0, has_side_effects=True, vmem_limit_bytes=56 * 1024 * 1024
        ),
        cost_estimate=pl.CostEstimate(flops=1_000_000_000, bytes_accessed=3_000_000, transcendentals=1_600_000),
    )

    def device(tokens, norm_gain, qkv_weight, proj_weight, rel_bias, cotangent):
        def inside(grid):
            return grid.transpose(1, 2, 0, 3).reshape(local)

        def outside(slabs):
            return slabs.reshape(ROWS, COLS, FRAMES, C).transpose(2, 0, 1, 3)

        block_out, token_grad, proj_grad = call(
            inside(tokens), norm_gain.reshape(1, C), qkv_weight, proj_weight, rel_bias, inside(cotangent)
        )
        return outside(block_out), outside(token_grad), proj_grad.T

    whole = P("tm", "height", None, None)
    return jax.shard_map(
        device,
        mesh=mesh,
        in_specs=(whole, P(), P(), P(), P(), whole),
        out_specs=(whole, whole, P(None, "height")),
        check_vma=False,
    )
```
